256 devices in a mesh: sp: 16 (over z, y_lo), fsdp: 16 (over y_hi, x, core).
Axes of the slice: x: 4, y: 4 (y_hi: 2, y_lo: 2; y = y_hi * 2 + y_lo), z: 8, core: 2. Of those that a mesh axis runs over, the one named last changes fastest.
Arguments:
- query_states: bfloat16 [16, 2048, 4096], P('fsdp', 'sp'), may hold values from -6 to 6
- key_states: bfloat16 [16, 2048, 512], P('fsdp', 'sp'), may hold values from -6 to 6
- forward_value_states: bfloat16 [16, 2048, 512], P('fsdp', 'sp'), may hold values from -6 to 6
- grad_output: bfloat16 [16, 2048, 4096], P('fsdp', 'sp'), may hold values from -6 to 6
- layer_input: bfloat16 [16, 2048, 5120], P('fsdp', 'sp'), may hold values from -6 to 6
- segment_ids: int32 [16, 2048], P('fsdp'), may hold values from 0 to 3, never falling along the last dimension, each value on 1 to 1024 neighbouring positions
Outputs:
- grad_query: bfloat16 [16, 2048, 4096], P('fsdp', 'sp')
- grad_key: bfloat16 [16, 2048, 512], P('fsdp', 'sp')
- grad_value_weight: float32 [5120, 512], P(('sp', 'fsdp'))
The draws below stay inside these ranges and needn't reach their ends.
Inputs may be any that keep to these rules, and one draw needn't show every extreme that they name: `segment_ids`: in each sequence the rollout numbers never fall; every rollout has 1 to 1024 positions and one has exactly 1024.
All inputs are finite; a program needn't handle non-finite values.
Results may differ from the reference program's by a relative error of at most 0.012.
Values may be sent and summed in bfloat16 or wider, within the bound.
No kernel may reach another device: no remote copies, remote signals or barrier semaphores. Data moves between devices by JAX's collectives and lax.ppermute only.
A program may use at most 128 MiB of HBM per device.

```python
import math
import jax
import jax.numpy as jnp
import numpy as np
from jax import lax

D = 5120
QUERY_HEAD_COUNT = 32
KEY_VALUE_HEADS = 4
HEAD_SIZE = 128
ROLLOUTS = 4
SEQUENCE_LENGTH = 2048
SEQUENCE_COUNT = 16


def draw_query_states(key, part):
    key = jax.random.fold_in(key, 11)
    base_offset = jnp.clip(jax.random.normal(key, (SEQUENCE_COUNT, SEQUENCE_LENGTH, QUERY_HEAD_COUNT * HEAD_SIZE), jnp.float32), -6.0, 6.0)
    return base_offset.astype(jnp.bfloat16)


def draw_key_states(key, part):
    key = jax.random.fold_in(key, 23)
    base_offset = jnp.clip(jax.random.normal(key, (SEQUENCE_COUNT, SEQUENCE_LENGTH, KEY_VALUE_HEADS * HEAD_SIZE), jnp.float32), -6.0, 6.0)
    return base_offset.astype(jnp.bfloat16)


def raised(entries, stream_key, source, target, parts, factor):
    owner, partner = [(jnp.arange(entries.shape[axis_at]) // (entries.shape[axis_at] // parts)).reshape([-1 if axis == axis_at else 1 for axis in range(entries.ndim)]) for axis_at in (source, target)]
    chosen = jax.random.permutation(stream_key, parts)[partner]
    strong = (owner == chosen) | (owner == (partner + parts // 2) % parts)
    return jnp.where(strong, factor * entries, entries)


def steps_of(own_key, dims, cuts, smallest, high):
    loudness = 1.0
    for dim, shards_of in cuts:
        steps = jax.random.uniform(jax.random.fold_in(jax.random.fold_in(own_key, 6), dim), (shards_of,), jnp.float32, smallest / len(cuts), high / len(cuts))
        loudness = loudness * jnp.repeat(jnp.exp(steps), dims[dim] // shards_of).reshape((-1,) + (1,) * (len(dims) - 1 - dim))
    return loudness


def split_up(number_of, total, limit, skew):
    portions = [(1 << 20) // math.isqrt(rank ** skew) + 1 for rank in range(2, number_of + 1)]
    rest, holding = total - limit - (number_of - 1), [1] * (number_of - 1)
    while rest > 0:
        free = [i for i in range(number_of - 1) if holding[i] < limit]
        mass, budget = sum([portions[i] for i in free]), rest
        for i in free:
            extra = min(limit - holding[i], max(1, budget * portions[i] // mass), rest)
            holding[i] = holding[i] + extra
            rest = rest - extra
    return np.array([limit] + holding)


def ragged_sizes(rng, number_of, total, bound, lean):
    if number_of == 2:
        one = jax.random.randint(rng, (), max(1, total - bound), min(bound, total - 1) + 1)
        return jnp.stack([one, total - one])
    tallies = jnp.asarray(split_up(number_of, total, bound, lean), jnp.int32)
    pairs = (number_of - 1) // 2
    donor, sink = tallies[1:1 + 2 * pairs:2], tallies[2:2 + 2 * pairs:2]
    margin = jnp.minimum(donor - 1, bound - sink)
    shifted = jax.random.randint(jax.random.fold_in(rng, 1), (pairs,), 0, 1 << 20) % (margin + 1)
    tallies = tallies.at[1:1 + 2 * pairs:2].set(donor - shifted).at[2:2 + 2 * pairs:2].set(sink + shifted)
    return tallies[jax.random.permutation(jax.random.fold_in(rng, 2), number_of)]


def scatter_about(own_key, dims, spread, reach, pieces=(), kind=jnp.bfloat16):
    result = jax.random.normal(own_key, dims, jnp.float32) * spread
    if len(pieces) > 0:
        result = steps_of(own_key, dims, pieces, -0.22, 0.18) * result
    return jnp.clip(result, min=-reach, max=reach).astype(kind)


def heavy_noise(key, dims, width, most, pieces, heavy, held_as=jnp.bfloat16):
    drawn = width * jax.random.normal(key, dims, jnp.float32)
    if pieces:
        drawn = drawn * steps_of(key, dims, pieces, -0.22, 0.18)
    return jnp.clip(raised(drawn, jax.random.fold_in(key, 3), *heavy), -most, most).astype(held_as)


def setup_inputs(seed: int = 0) -> dict:
    keys = jax.random.split(jax.random.key(seed), 7)
    return {
        "query_states": draw_query_states(jax.random.fold_in(keys[6], 71), 0),
        "key_states": draw_key_states(jax.random.fold_in(keys[6], 71), 0),
        "forward_value_states": scatter_about(keys[2], (SEQUENCE_COUNT, SEQUENCE_LENGTH, KEY_VALUE_HEADS * HEAD_SIZE), 1.0, 6.0, ((0, 16), (1, 16))),
        "grad_output": scatter_about(keys[3], (SEQUENCE_COUNT, SEQUENCE_LENGTH, QUERY_HEAD_COUNT * HEAD_SIZE), 1.0, 6.0, ((0, 16), (1, 16))),
        "layer_input": heavy_noise(keys[4], (SEQUENCE_COUNT, SEQUENCE_LENGTH, D), 1.0, 6.0, ((0, 16), (1, 16)), (1, 2, 16, 2.0)),
        "segment_ids": jax.vmap(lambda own: jnp.searchsorted(jnp.cumsum(ragged_sizes(own, ROLLOUTS, SEQUENCE_LENGTH, SEQUENCE_LENGTH // 2, 1)), jnp.arange(SEQUENCE_LENGTH), side="right"))(jax.random.split(keys[5], SEQUENCE_COUNT)).reshape((SEQUENCE_COUNT, SEQUENCE_LENGTH)).astype(jnp.int32),
    }


def head_backward(query_head, key_group, value_group, grad_head, allowed):
    softmax_scale = 1.0 / math.sqrt(HEAD_SIZE)
    scores = jnp.dot(query_head, key_group.T, preferred_element_type=jnp.float32) * softmax_scale
    scores = jnp.where(allowed, scores, -jnp.inf)
    largest = lax.optimization_barrier(jnp.max(scores, axis=1, keepdims=True))
    weights = jnp.exp(scores - largest)
    weights = weights / lax.optimization_barrier(jnp.sum(weights, axis=1, keepdims=True))
    weights_low = weights.astype(jnp.bfloat16)
    attended = jnp.dot(weights_low, value_group, preferred_element_type=jnp.float32)
    row_terms = lax.optimization_barrier(jnp.sum(grad_head.astype(jnp.float32) * attended, axis=1, keepdims=True))
    grad_weights = jnp.dot(grad_head, value_group.T, preferred_element_type=jnp.float32)
    grad_scores = (weights * (grad_weights - row_terms)).astype(jnp.bfloat16)
    grad_query = (jnp.dot(grad_scores, key_group, preferred_element_type=jnp.float32) * softmax_scale).astype(jnp.bfloat16)
    grad_key = jnp.dot(grad_scores.T, query_head, preferred_element_type=jnp.float32) * softmax_scale
    grad_value = jnp.dot(weights_low.T, grad_head, preferred_element_type=jnp.float32)
    return (grad_query, grad_key, grad_value)

def one_sequence(operands):
    query_row_block, key_row_block, value_row_block, gradient_rows, segment_row = operands
    token_length = query_row_block.shape[0]
    group_width = QUERY_HEAD_COUNT // KEY_VALUE_HEADS
    positions = jnp.arange(token_length, dtype=jnp.int32)
    allowed = (segment_row[:, None] == segment_row[None, :]) & (positions[None, :] <= positions[:, None])
    query_head_groups = query_row_block.reshape(token_length, KEY_VALUE_HEADS, group_width, HEAD_SIZE).transpose(1, 2, 0, 3)
    gradient_groups = gradient_rows.reshape(token_length, KEY_VALUE_HEADS, group_width, HEAD_SIZE).transpose(1, 2, 0, 3)
    key_head_groups = key_row_block.reshape(token_length, KEY_VALUE_HEADS, HEAD_SIZE).transpose(1, 0, 2)
    value_head_groups = value_row_block.reshape(token_length, KEY_VALUE_HEADS, HEAD_SIZE).transpose(1, 0, 2)

    def one_group(group_operands):
        query_set, key_group, value_group, grad_set = group_operands

        def one_head(carry, head_operands):
            query_head, grad_head = head_operands
            grad_query, grad_key, grad_value = head_backward(query_head, key_group, value_group, grad_head, allowed)
            return ((carry[0] + grad_key, carry[1] + grad_value), grad_query)
        empty = jnp.zeros((token_length, HEAD_SIZE), jnp.float32)
        totals, grad_queries = lax.scan(one_head, (empty, empty), (query_set, grad_set))
        return (grad_queries, totals[0], totals[1])
    grad_queries, key_partial_sums, value_partial_sums = lax.map(one_group, (query_head_groups, key_head_groups, value_head_groups, gradient_groups))
    grad_queries = grad_queries.transpose(2, 0, 1, 3).reshape(token_length, QUERY_HEAD_COUNT * HEAD_SIZE)
    key_partial_sums = key_partial_sums.transpose(1, 0, 2).reshape(token_length, KEY_VALUE_HEADS * HEAD_SIZE)
    value_partial_sums = value_partial_sums.transpose(1, 0, 2).reshape(token_length, KEY_VALUE_HEADS * HEAD_SIZE)
    return (grad_queries, key_partial_sums.astype(jnp.bfloat16), value_partial_sums.astype(jnp.bfloat16))

def reference(query_states, key_states, forward_value_states, grad_output, layer_input, segment_ids):
    grad_query, grad_key, value_reduced_precision = lax.map(one_sequence, (query_states, key_states, forward_value_states, grad_output, segment_ids))
    flat_input = layer_input.reshape(-1, D)
    flattened_value = value_reduced_precision.reshape(-1, KEY_VALUE_HEADS * HEAD_SIZE)
    weight_grad = jnp.dot(flat_input.T, flattened_value, preferred_element_type=jnp.float32)
    weight_grad = weight_grad * (1.0 / math.sqrt(flat_input.shape[0]))
    return (grad_query, grad_key, weight_grad)
```

```python
import functools
import math

import jax
import jax.numpy as jnp
from jax import lax
from jax.experimental import pallas as pl
from jax.experimental.pallas import tpu as pltpu
from jax.sharding import Mesh
from jax.sharding import PartitionSpec as P

HEAD = 128
SCALE = 1.0 / math.sqrt(HEAD)
LOG2E = math.log2(math.e)
BF = jnp.bfloat16
F32 = jnp.float32
BACK = 4
TOK = 128
BLK = 256
WIN = (BACK + 1) * BLK
VMEM = 56 * 1024 * 1024
NT = (((1,), (1,)), ((), ()))


def heads_of(own_ref, recv_ref, count):
    rows = []
    for h in range(count):
        cols = slice(h * HEAD, (h + 1) * HEAD)
        rows += [own_ref[:, cols], recv_ref[:, cols]]
    return jnp.concatenate(rows, axis=0)


def probs_kernel(s_ref, qo, qr, go, gr, k0, k1, k2, k3, k4, bias, probs, d0, d1, d2, d3, d4, acc):
    step = pl.program_id(1)
    keys = jnp.concatenate([k[...] for k in (k0, k1, k2, k3, k4)], axis=0)
    queries = heads_of(qo, qr, 2)
    scores = lax.dot_general(keys, queries, NT, preferred_element_type=F32)
    for h in range(2):
        t = scores[:, h * BLK : (h + 1) * BLK] * (SCALE * LOG2E) + bias[...]
        e = jnp.exp2(t - jnp.max(t, axis=0, keepdims=True))
        p = e * (1.0 / jnp.sum(e, axis=0, keepdims=True))
        probs[0, 0, :, h * BLK : (h + 1) * BLK] = p.astype(BF)
    part = jnp.dot(probs[0, 0], heads_of(go, gr, 2), preferred_element_type=F32)

    @pl.when(step == 0)
    def _():
        acc[...] = part

    @pl.when(step > 0)
    def _():
        acc[...] += part

    @pl.when(step == pl.num_programs(1) - 1)
    def _():
        for i, out in enumerate((d0, d1, d2, d3, d4)):
            out[...] = acc[i * BLK : (i + 1) * BLK, :].astype(out.dtype)


def grads_kernel(
    s_ref, qo, qr, go, gr, k0, k1, k2, k3, k4, v0, v1, v2, v3, v4, probs,
    dqo, dqr, d0, d1, d2, d3, d4, acc, key_t,
):
    step = pl.program_id(1)

    @pl.when(step == 0)
    def _():
        for i, k in enumerate((k0, k1, k2, k3, k4)):
            key_t[:, i * BLK : (i + 1) * BLK] = k[...].T

    values = jnp.concatenate([v[...] for v in (v0, v1, v2, v3, v4)], axis=0)
    grad_probs = lax.dot_general(values, heads_of(go, gr, 2), NT, preferred_element_type=F32)
    p = probs[0, 0].astype(F32)
    row_terms = jnp.sum(p * grad_probs, axis=0, keepdims=True)
    ds = (p * (grad_probs - row_terms)).astype(BF)
    part = jnp.dot(ds, heads_of(qo, qr, 2), preferred_element_type=F32)
    dq = (jnp.dot(key_t[...], ds, preferred_element_type=F32) * SCALE).T.astype(BF)
    for h in range(2):
        cols = slice(h * HEAD, (h + 1) * HEAD)
        dqo[:, cols] = dq[h * BLK : h * BLK + TOK]
        dqr[:, cols] = dq[h * BLK + TOK : (h + 1) * BLK]

    @pl.when(step == 0)
    def _():
        acc[...] = part

    @pl.when(step > 0)
    def _():
        acc[...] += part

    @pl.when(step == pl.num_programs(1) - 1)
    def _():
        for i, out in enumerate((d0, d1, d2, d3, d4)):
            out[...] = (acc[i * BLK : (i + 1) * BLK, :] * SCALE).astype(out.dtype)


def own_spec():
    return pl.BlockSpec((TOK, 2 * HEAD), lambda j, i, s: (0, s[0] * 8 + j * 4 + i))


def recv_spec():
    return pl.BlockSpec((TOK, 2 * HEAD), lambda j, i, s: (0, j * 4 + i))


def block_spec():
    return pl.BlockSpec((BLK, HEAD), lambda j, i, s: (0, j))


def probs_spec():
    return pl.BlockSpec((1, 1, WIN, 2 * BLK), lambda j, i, s: (j, i, 0, 0))


def window_outs():
    first = jax.ShapeDtypeStruct((BLK, 2 * HEAD), F32)
    return [first] + [jax.ShapeDtypeStruct((BLK, 2 * HEAD), BF)] * BACK


def run_probs(place, qo, qr, go, gr, keys, bias):
    flops = 2 * 2 * 16 * WIN * BLK * HEAD
    outs = pl.pallas_call(
        probs_kernel,
        grid_spec=pltpu.PrefetchScalarGridSpec(
            num_scalar_prefetch=1,
            grid=(2, 4),
            in_specs=[own_spec(), recv_spec(), own_spec(), recv_spec()]
            + [block_spec()] * (BACK + 1)
            + [pl.BlockSpec((WIN, BLK), lambda j, i, s: (0, 0))],
            out_specs=[probs_spec()] + [block_spec()] * (BACK + 1),
            scratch_shapes=[pltpu.VMEM((WIN, HEAD), F32)],
        ),
        out_shape=[jax.ShapeDtypeStruct((2, 4, WIN, 2 * BLK), BF)] + window_outs(),
        compiler_params=pltpu.CompilerParams(vmem_limit_bytes=VMEM),
        cost_estimate=pl.CostEstimate(
            flops=flops, bytes_accessed=16 << 20, transcendentals=16 * WIN * BLK
        ),
        name="probs",
    )(place, qo, qr, go, gr, *keys, bias)
    return outs[0], outs[1:]


def run_grads(place, qo, qr, go, gr, keys, values, probs):
    flops = 3 * 2 * 16 * WIN * BLK * HEAD
    outs = pl.pallas_call(
        grads_kernel,
        grid_spec=pltpu.PrefetchScalarGridSpec(
            num_scalar_prefetch=1,
            grid=(2, 4),
            in_specs=[own_spec(), recv_spec(), own_spec(), recv_spec()]
            + [block_spec()] * (2 * BACK + 2)
            + [probs_spec()],
            out_specs=[recv_spec(), recv_spec()] + [block_spec()] * (BACK + 1),
            scratch_shapes=[pltpu.VMEM((WIN, HEAD), F32), pltpu.VMEM((HEAD, WIN), BF)],
        ),
        out_shape=[jax.ShapeDtypeStruct((TOK, 16 * HEAD), BF)] * 2 + window_outs(),
        compiler_params=pltpu.CompilerParams(vmem_limit_bytes=VMEM),
        cost_estimate=pl.CostEstimate(flops=flops, bytes_accessed=16 << 20, transcendentals=0),
        name="grads",
    )(place, qo, qr, go, gr, *keys, *values, probs)
    return outs[0], outs[1], outs[2:]


def weight_kernel(s_ref, xo, xr, mine, theirs, out):
    x, c = s_ref[1], s_ref[2]
    total = jnp.zeros(out.shape, F32)
    for other, ref in ((0, mine), (1, theirs)):
        core = c if other == 0 else 1 - c
        for d in range(4):
            seq = lax.rem(x - d + 4, 4) * 2 + core
            total += jnp.dot(xo[seq], ref[d, :TOK], preferred_element_type=F32)
            total += jnp.dot(xr[seq], ref[d, TOK:], preferred_element_type=F32)
    out[...] = total.astype(out.dtype)


def run_weight(place, xo, xr, mine, theirs):
    whole = pl.BlockSpec(memory_space=pltpu.VMEM)
    return pl.pallas_call(
        weight_kernel,
        in_specs=[pl.BlockSpec(memory_space=pltpu.SMEM)] + [whole] * 4,
        out_specs=whole,
        out_shape=jax.ShapeDtypeStruct((xo.shape[1], 2 * HEAD), BF),
        compiler_params=pltpu.CompilerParams(vmem_limit_bytes=VMEM),
        cost_estimate=pl.CostEstimate(
            flops=2 * 2048 * 640 * 256, bytes_accessed=4 << 20, transcendentals=0
        ),
        name="weight",
    )(place, xo, xr, mine, theirs)


def body(sizes, query, key, value, grad, layer_input, segment_ids):
    nz = sizes["z"]
    z, yl, x, c = (lax.axis_index(a) for a in ("z", "yl", "x", "c"))
    place = jnp.stack([yl, x, c]).astype(jnp.int32)
    q, k, v, g, xin, seg = (a[0] for a in (query, key, value, grad, layer_input, segment_ids))
    swap = [(0, 1), (1, 0)]

    def half(a, which, width):
        return lax.dynamic_slice_in_dim(a, which * width, width, 1)

    def to_pair(a):
        return lax.ppermute(a, "yl", swap)

    keys = [jnp.concatenate([half(k, yl, 256), to_pair(half(k, 1 - yl, 256))], 0)]
    values = [jnp.concatenate([half(v, yl, 256), to_pair(half(v, 1 - yl, 256))], 0)]
    q_recv = to_pair(half(q, 1 - yl, 2048))
    g_recv = to_pair(half(g, 1 - yl, 2048))
    onward = [(i, i + 1) for i in range(nz - 1)]
    for _ in range(BACK):
        keys.append(lax.ppermute(keys[-1], "z", onward))
        values.append(lax.ppermute(values[-1], "z", onward))

    groups = 8
    x_t = xin.T
    width = x_t.shape[0] // groups
    x_own = lax.all_to_all(x_t, ("x", "c"), split_axis=0, concat_axis=0, tiled=True)
    x_own = x_own.reshape(groups, width, TOK)
    x_recv = to_pair(x_own)

    offset = jnp.arange(TOK, dtype=jnp.int32)
    within = jnp.concatenate([yl * TOK + offset, (1 - yl) * TOK + offset])
    key_pos = ((z - jnp.arange(BACK + 1, dtype=jnp.int32))[:, None] * BLK + within[None]).reshape(WIN)
    query_pos = z * BLK + within
    padded = jnp.concatenate([jnp.full((BACK * BLK,), -1, jnp.int32), seg])
    window = lax.dynamic_slice_in_dim(padded, z * BLK, WIN).reshape(BACK + 1, 2, TOK)[::-1]
    window = jnp.where(yl == 0, window, window[:, ::-1])
    query_seg = window[0].reshape(BLK)
    allowed = (window.reshape(WIN)[:, None] == query_seg[None]) & (
        key_pos[:, None] <= query_pos[None]
    )
    bias = jnp.where(allowed, 0.0, -jnp.inf).astype(F32)

    def home(parts):
        total = parts[0]
        for d in range(1, BACK + 1):
            back = [(i, i - d) for i in range(d, nz)]
            total = total + lax.ppermute(parts[d], "z", back).astype(F32)
        return total.astype(BF)

    probs, value_parts = run_probs(place, q, q_recv, g, g_recv, keys, bias)
    value_low = home(value_parts)
    dq_own, dq_far, key_parts = run_grads(place, q, q_recv, g, g_recv, keys, values, probs)

    near = [value_low]
    for d in range(1, 4):
        near.append(lax.ppermute(value_low, "x", [(i, (i + d) % 4) for i in range(4)]))
    near = jnp.stack(near)
    far = lax.ppermute(near, "c", swap)
    part = run_weight(place, x_own, x_recv, near, far)
    rows = width // 32
    part = lax.all_to_all(
        part.reshape(32, rows, 256), ("z", "yl", "yh"), split_axis=0, concat_axis=0, tiled=True
    )
    total = part.reshape(nz, 2, 2, rows, 256).astype(F32).sum(axis=(0, 2))
    total = jnp.concatenate([total[0], total[1]], axis=1)
    total = total * (1.0 / math.sqrt(16 * 2048))
    moves = []
    for i in range(256):
        zy, xi, ci = i // 8, (i % 8) // 2, i % 2
        moves.append((i, (xi * 2 + ci) * 32 + zy))
    weight = lax.ppermute(total, ("z", "yl", "yh", "x", "c"), moves)

    def join(mine, theirs):
        return jnp.where(
            yl == 0,
            jnp.concatenate([mine, theirs], 1),
            jnp.concatenate([theirs, mine], 1),
        )

    dq = join(dq_own, to_pair(dq_far))
    key_low = home(key_parts)
    dk = join(key_low[:TOK], to_pair(key_low[TOK:]))
    return dq[None], dk[None], weight


def solution(mesh):
    fine = Mesh(mesh.devices.reshape(8, 2, 2, 4, 2), ("z", "yl", "yh", "x", "c"))
    sizes = dict(fine.shape)
    tokens = P(("yh", "x", "c"), ("z", "yl"), None)
    return jax.shard_map(
        functools.partial(body, sizes),
        mesh=fine,
        in_specs=(tokens,) * 5 + (P(("yh", "x", "c"), None),),
        out_specs=(tokens, tokens, P(("z", "yl", "yh", "x", "c"), None)),
        check_vma=False,
    )
```

```python
import functools
import math

import jax
import jax.numpy as jnp
from jax import lax
from jax.experimental import pallas as pl
from jax.experimental.pallas import tpu as pltpu
from jax.sharding import Mesh
from jax.sharding import PartitionSpec as P

HEAD = 128
SCALE = 1.0 / math.sqrt(HEAD)
BF = jnp.bfloat16
F32 = jnp.float32
BACK = 4
TOK = 128
BLK = 256
WIN = (BACK + 1) * BLK
GROUP = 8
ROWS = GROUP * BLK
CHUNK = 64
VMEM = 56 * 1024 * 1024
FAR = -(2.0**100)
NT = (((1,), (1,)), ((), ()))


def heads_of(own_ref, recv_ref):
    rows = []
    for h in range(GROUP):
        cols = slice(h * HEAD, (h + 1) * HEAD)
        rows += [own_ref[:, cols], recv_ref[:, cols]]
    return jnp.concatenate(rows, axis=0)


def fold(a, op):
    return op(a.reshape(a.shape[0] // 8, 8, a.shape[1]), axis=0)


def chunks():
    return [slice(c, c + CHUNK) for c in range(0, WIN, CHUNK)]


def score_all(qo, qr, blocks, key_code, query_code, tri, keys, queries, scores):
    for i, k in enumerate(blocks):
        keys[i * BLK : (i + 1) * BLK, :HEAD] = k[...]
    keys[:, HEAD:] = key_code[...]
    queries[:, :HEAD] = heads_of(qo, qr)
    for h in range(GROUP):
        queries[h * BLK : (h + 1) * BLK, HEAD:] = query_code[...]
    scores[...] = lax.dot_general(keys[...], queries[...], NT, preferred_element_type=F32)
    scores[:BLK] += jnp.concatenate([tri[...]] * GROUP, 1)


def probs_kernel(
    s_ref, qo, qr, go, gr, k0, k1, k2, k3, k4, key_code, query_code, tri,
    shift, d0, d1, d2, d3, d4, keys, queries, scores, weights,
):
    score_all(qo, qr, (k0, k1, k2, k3, k4), key_code, query_code, tri, keys, queries, scores)
    largest = jnp.full((8, ROWS), -jnp.inf, F32)
    for rows in chunks():
        largest = jnp.maximum(largest, fold(scores[rows], jnp.max))
    largest = jnp.max(largest, axis=0, keepdims=True)
    total = jnp.zeros((8, ROWS), F32)
    for rows in chunks():
        e = jnp.exp((scores[rows] - largest) * SCALE)
        total += fold(e, jnp.sum)
        weights[rows] = e.astype(BF)
    total = jnp.sum(total, axis=0, keepdims=True)
    shift[0] = jnp.broadcast_to(largest * SCALE + jnp.log(total), (8, ROWS))
    inverse = jnp.broadcast_to(1.0 / total, (8, ROWS)).T[:, :1]
    g = (heads_of(go, gr).astype(F32) * inverse).astype(BF)
    part = jnp.dot(weights[...], g, preferred_element_type=F32)
    for i, out in enumerate((d0, d1, d2, d3, d4)):
        out[...] = part[i * BLK : (i + 1) * BLK].astype(out.dtype)


def grads_kernel(
    s_ref, qo, qr, go, gr, k0, k1, k2, k3, k4, v0, v1, v2, v3, v4, key_code, query_code, tri, shift,
    dqo, dqr, d0, d1, d2, d3, d4, keys, queries, scores, key_t, values, grad_probs, grad_scores,
):
    score_all(qo, qr, (k0, k1, k2, k3, k4), key_code, query_code, tri, keys, queries, scores)
    for i, (k, v) in enumerate(zip((k0, k1, k2, k3, k4), (v0, v1, v2, v3, v4))):
        key_t[:, i * BLK : (i + 1) * BLK] = k[...].T
        values[i * BLK : (i + 1) * BLK] = v[...]
    grad_probs[...] = lax.dot_general(
        values[...], heads_of(go, gr), NT, preferred_element_type=F32
    )
    row_terms = jnp.zeros((8, ROWS), F32)
    for rows in chunks():
        p = jnp.exp(scores[rows] * SCALE - shift[0, :1])
        scores[rows] = p
        row_terms += fold(p * grad_probs[rows], jnp.sum)
    row_terms = jnp.sum(row_terms, axis=0, keepdims=True)
    for rows in chunks():
        grad_scores[rows] = (scores[rows] * (grad_probs[rows] - row_terms)).astype(BF)
    part = jnp.dot(grad_scores[...], heads_of(qo, qr), preferred_element_type=F32)
    dq = jnp.dot(key_t[...], grad_scores[...], preferred_element_type=F32)
    dq = (dq * SCALE).T.astype(BF)
    for h in range(GROUP):
        cols = slice(h * HEAD, (h + 1) * HEAD)
        dqo[:, cols] = dq[h * BLK : h * BLK + TOK]
        dqr[:, cols] = dq[h * BLK + TOK : (h + 1) * BLK]
    for i, out in enumerate((d0, d1, d2, d3, d4)):
        out[...] = (part[i * BLK : (i + 1) * BLK] * SCALE).astype(out.dtype)


def own_spec():
    return pl.BlockSpec((TOK, GROUP * HEAD), lambda j, s: (0, s[0] * 2 + j))


def recv_spec():
    return pl.BlockSpec((TOK, GROUP * HEAD), lambda j, s: (0, j))


def window_specs():
    second = pl.BlockSpec((BLK, HEAD), lambda j, s: (1, j))
    return [block_spec(), block_spec(), block_spec(), second, block_spec()]


def block_spec():
    return pl.BlockSpec((BLK, HEAD), lambda j, s: (0, j))


def same_spec(*shape):
    return pl.BlockSpec(shape, lambda j, s: (0, 0))


def shift_spec():
    return pl.BlockSpec((1, 8, ROWS), lambda j, s: (j, 0, 0))


def code_specs():
    return [same_spec(WIN, HEAD), same_spec(BLK, HEAD), same_spec(BLK, BLK)]


def score_scratch():
    return [
        pltpu.VMEM((WIN, 2 * HEAD), BF),
        pltpu.VMEM((ROWS, 2 * HEAD), BF),
        pltpu.VMEM((WIN, ROWS), F32),
    ]


def vmem_spec():
    return pl.BlockSpec(memory_space=pltpu.VMEM)


def window_outs():
    first = jax.ShapeDtypeStruct((BLK, 2 * HEAD), F32)
    return [first] + [jax.ShapeDtypeStruct((BLK, 2 * HEAD), BF)] * BACK


def run_probs(place, qo, qr, go, gr, keys, codes):
    outs = pl.pallas_call(
        probs_kernel,
        grid_spec=pltpu.PrefetchScalarGridSpec(
            num_scalar_prefetch=1,
            grid=(2,),
            in_specs=[own_spec(), recv_spec(), own_spec(), recv_spec()]
            + window_specs()
            + code_specs(),
            out_specs=[shift_spec()] + [block_spec()] * (BACK + 1),
            scratch_shapes=score_scratch() + [pltpu.VMEM((WIN, ROWS), BF)],
        ),
        out_shape=[jax.ShapeDtypeStruct((2, 8, ROWS), F32)] + window_outs(),
        compiler_params=pltpu.CompilerParams(vmem_limit_bytes=VMEM),
        cost_estimate=pl.CostEstimate(
            flops=2 * 3 * 16 * WIN * BLK * HEAD,
            bytes_accessed=16 << 20,
            transcendentals=16 * WIN * BLK,
        ),
        name="probs",
    )(place, qo, qr, go, gr, *keys, *codes)
    return outs[0], outs[1:]


def run_grads(place, qo, qr, go, gr, keys, values, codes, shift):
    outs = pl.pallas_call(
        grads_kernel,
        grid_spec=pltpu.PrefetchScalarGridSpec(
            num_scalar_prefetch=1,
            grid=(2,),
            in_specs=[own_spec(), recv_spec(), own_spec(), recv_spec()]
            + window_specs()
            + window_specs()
            + code_specs()
            + [shift_spec()],
            out_specs=[recv_spec(), recv_spec()] + [block_spec()] * (BACK + 1),
            scratch_shapes=score_scratch()
            + [
                pltpu.VMEM((HEAD, WIN), BF),
                pltpu.VMEM((WIN, HEAD), BF),
                pltpu.VMEM((WIN, ROWS), F32),
                pltpu.VMEM((WIN, ROWS), BF),
            ],
        ),
        out_shape=[jax.ShapeDtypeStruct((TOK, 16 * HEAD), BF)] * 2 + window_outs(),
        compiler_params=pltpu.CompilerParams(vmem_limit_bytes=VMEM),
        cost_estimate=pl.CostEstimate(
            flops=2 * 5 * 16 * WIN * BLK * HEAD,
            bytes_accessed=16 << 20,
            transcendentals=16 * WIN * BLK,
        ),
        name="grads",
    )(place, qo, qr, go, gr, *keys, *values, *codes, shift)
    return outs[0], outs[1], outs[2:]


def weight_kernel(s_ref, xo, xr, mine, theirs, out):
    x, c = s_ref[1], s_ref[2]
    total = jnp.zeros((xo.shape[1], 2 * HEAD), F32)
    for other, ref in ((0, mine), (1, theirs)):
        core = c if other == 0 else 1 - c
        for d in range(4):
            seq = lax.rem(x - d + 4, 4) * 2 + core
            total += jnp.dot(xo[seq], ref[d, :TOK], preferred_element_type=F32)
            total += jnp.dot(xr[seq], ref[d, TOK:], preferred_element_type=F32)
    out[...] = total.astype(out.dtype)


def run_weight(place, xo, xr, mine, theirs):
    return pl.pallas_call(
        weight_kernel,
        in_specs=[pl.BlockSpec(memory_space=pltpu.SMEM)] + [vmem_spec()] * 4,
        out_specs=vmem_spec(),
        out_shape=jax.ShapeDtypeStruct((xo.shape[1], 2 * HEAD), BF),
        compiler_params=pltpu.CompilerParams(vmem_limit_bytes=16 << 20),
        cost_estimate=pl.CostEstimate(
            flops=2 * 2048 * 640 * 256, bytes_accessed=4 << 20, transcendentals=0
        ),
        name="weight",
    )(place, xo, xr, mine, theirs)


def after(value, *others):
    return lax.optimization_barrier((value, *others))


def small_call(kernel, out_shape, name, args, tokens=()):
    def run(*refs):
        kernel(*refs[: len(args)], *refs[len(args) + len(tokens) :])

    return pl.pallas_call(
        run,
        in_specs=[vmem_spec()] * len(args) + [pl.BlockSpec(memory_space=pl.ANY)] * len(tokens),
        out_specs=vmem_spec(),
        out_shape=out_shape,
        compiler_params=pltpu.CompilerParams(vmem_limit_bytes=16 << 20),
        cost_estimate=pl.CostEstimate(flops=0, bytes_accessed=2 << 20, transcendentals=0),
        name=name,
    )(*args, *tokens)


def sum_kernel(first, a, b, c, d, out):
    total = first[...] + a[...].astype(F32) + b[...].astype(F32)
    out[...] = (total + c[...].astype(F32) + d[...].astype(F32)).astype(BF)


def body(sizes, query, key, value, grad, layer_input, segment_ids):
    nz = sizes["z"]
    z, yl, x, c = (lax.axis_index(a) for a in ("z", "yl", "x", "c"))
    place = jnp.stack([yl, x, c, z]).astype(jnp.int32)
    q, k, v, g, xin, seg = (a[0] for a in (query, key, value, grad, layer_input, segment_ids))
    swap = [(0, 1), (1, 0)]

    def half(a, which, width):
        return lax.dynamic_slice_in_dim(a, which * width, width, 1)

    def to_pair(a):
        return lax.ppermute(a, "yl", swap)

    kv_send = jnp.concatenate([half(k, 1 - yl, 256), half(v, 1 - yl, 256)], 1)
    kv_send, q, g, xin = after(kv_send, q, g, xin)
    kv_recv = to_pair(kv_send)
    q_recv = to_pair(half(q, 1 - yl, 2048))
    g_recv = to_pair(half(g, 1 - yl, 2048))

    def fetch_first(own):
        one = lax.ppermute(own, "z", [(i, i + 1) for i in range(nz - 1)])
        round_first = [(i, (i - 2) % nz) for i in range(nz - BACK)]
        return one, lax.ppermute(own, "z", round_first)

    def fetch_rest(own, one, half_way):
        both = jnp.concatenate([own, one], 0)
        both = lax.ppermute(both, "z", [(i, i + 2) for i in range(nz - 2)])
        round_rest = [((i - 2) % nz, (i - 4) % nz) for i in range(nz - BACK)]
        return [own, one, both, both, lax.ppermute(half_way, "z", round_rest)]

    own_keys = jnp.concatenate([half(k, yl, 256), kv_recv[:, :256]], 0)
    own_values = jnp.concatenate([half(v, yl, 256), kv_recv[:, 256:]], 0)
    first_keys = fetch_first(own_keys)
    first_values = fetch_first(own_values)
    keys = fetch_rest(own_keys, *first_keys)
    values = fetch_rest(own_values, *first_values)

    groups = 8
    x_t = xin.T
    width = x_t.shape[0] // groups
    rows = width // 32
    x_t = x_t.reshape(32, groups, rows, TOK).transpose(1, 0, 2, 3).reshape(groups * width, TOK)
    x_own = lax.all_to_all(x_t, ("x", "c"), split_axis=0, concat_axis=0, tiled=True)
    x_own, q_recv, g_recv = after(x_own, q_recv, g_recv)
    x_own = x_own.reshape(groups, width, TOK)
    x_recv = to_pair(x_own)

    offset = jnp.arange(TOK, dtype=jnp.int32)
    within = jnp.concatenate([yl * TOK + offset, (1 - yl) * TOK + offset])
    padded = jnp.concatenate([jnp.full((BACK * BLK,), -1, jnp.int32), seg])
    window = lax.dynamic_slice_in_dim(padded, z * BLK, WIN).reshape(BACK + 1, 2, TOK)[::-1]
    window = jnp.where(yl == 0, window, window[:, ::-1])
    query_seg = window[0].reshape(BLK, 1)
    lanes = jnp.arange(HEAD, dtype=jnp.int32)[None]
    key_code = jnp.where((lanes < 4) & (window.reshape(WIN, 1) != lanes), FAR, 0.0).astype(BF)
    query_code = (query_seg == lanes).astype(BF)
    tri = jnp.where(within[:, None] <= within[None], 0.0, -jnp.inf).astype(F32)

    def travel(parts):
        sent = []
        for d in range(1, BACK + 1):
            sent.append(lax.ppermute(parts[d], "z", [(i, i - d) for i in range(d, nz)]))
        return sent

    def add_up(first, rest):
        for a in rest:
            first = first + a.astype(F32)
        return first.astype(BF)

    codes = (key_code, query_code, tri)
    shift, value_parts = run_probs(place, q, q_recv, g, g_recv, keys, codes)
    value_sent = travel(value_parts)
    dq_own, dq_far, key_parts = run_grads(
        place, q, q_recv, g, g_recv, keys, values, codes, shift
    )
    value_first, dq_far, key_parts, *value_sent = after(
        value_parts[0], dq_far, key_parts, *value_sent
    )
    value_low = add_up(value_first, value_sent)

    near = [value_low]
    for d in range(1, 4):
        near.append(lax.ppermute(value_low, "x", [(i, (i + d) % 4) for i in range(4)]))
    near = jnp.stack(near)
    far = lax.ppermute(near, "c", swap)
    part = run_weight(place, x_own, x_recv, near, far)
    dq_recv = to_pair(dq_far)
    key_sent = travel(key_parts)
    key_block = jax.ShapeDtypeStruct((BLK, 2 * HEAD), BF)
    key_low = small_call(sum_kernel, key_block, "key_sum", (key_parts[0], *key_sent), (part,))
    part = lax.all_to_all(
        part.reshape(32, rows, 256), ("z", "yl", "yh"), split_axis=0, concat_axis=0, tiled=True
    )
    total = part.reshape(nz, 2, 2, rows, 256).astype(F32).sum(axis=(0, 2))
    total = jnp.concatenate([total[0], total[1]], axis=1)
    weight = total * (1.0 / math.sqrt(16 * 2048))

    def join(mine, theirs):
        return jnp.where(
            yl == 0,
            jnp.concatenate([mine, theirs], 1),
            jnp.concatenate([theirs, mine], 1),
        )

    dq = join(dq_own, dq_recv)
    dk = join(key_low[:TOK], to_pair(key_low[TOK:]))
    return dq[None], dk[None], weight


def solution(mesh):
    fine = Mesh(mesh.devices.reshape(8, 2, 2, 4, 2), ("z", "yl", "yh", "x", "c"))
    sizes = dict(fine.shape)
    tokens = P(("yh", "x", "c"), ("z", "yl"), None)
    return jax.shard_map(
        functools.partial(body, sizes),
        mesh=fine,
        in_specs=(tokens,) * 5 + (P(("yh", "x", "c"), None),),
        out_specs=(tokens, tokens, P(("z", "yl", "yh", "x", "c"), None)),
        check_vma=False,
    )
```

```python
import functools
import math

import jax
import jax.numpy as jnp
from jax import lax
from jax.experimental import pallas as pl
from jax.experimental.pallas import tpu as pltpu
from jax.sharding import Mesh
from jax.sharding import PartitionSpec as P

HEAD = 128
SCALE = 1.0 / math.sqrt(HEAD)
BF = jnp.bfloat16
F32 = jnp.float32
BACK = 4
TOK = 128
BLK = 256
WIN = (BACK + 1) * BLK
GROUP = 8
ROWS = GROUP * BLK
CHUNK = 64
VMEM = 56 * 1024 * 1024
FAR = -(2.0**100)
NT = (((1,), (1,)), ((), ()))


def heads_of(own_ref, recv_ref):
    rows = []
    for h in range(GROUP):
        cols = slice(h * HEAD, (h + 1) * HEAD)
        rows += [own_ref[:, cols], recv_ref[:, cols]]
    return jnp.concatenate(rows, axis=0)


def fold(a, op):
    return op(a.reshape(a.shape[0] // 8, 8, a.shape[1]), axis=0)


def chunks():
    return [slice(c, c + CHUNK) for c in range(0, WIN, CHUNK)]


def score_all(s_ref, qo, qr, blocks, key_seg, query_seg, keys, queries, scores):
    lanes = lax.broadcasted_iota(jnp.int32, (1, HEAD), 1)
    for i, k in enumerate(blocks):
        rows = slice(i * BLK, (i + 1) * BLK)
        keys[rows, :HEAD] = k[...]
        seg = jnp.broadcast_to(key_seg[:, rows], (8, BLK)).T[:, :1]
        keys[rows, HEAD:] = jnp.where((lanes < 4) & (seg != lanes), FAR, 0.0).astype(BF)
    queries[:, :HEAD] = heads_of(qo, qr)
    query_code = jnp.broadcast_to(query_seg[...], (8, BLK)).T[:, :1] == lanes
    query_code = query_code.astype(BF)
    for h in range(GROUP):
        queries[h * BLK : (h + 1) * BLK, HEAD:] = query_code
    scores[...] = lax.dot_general(keys[...], queries[...], NT, preferred_element_type=F32)
    row = lax.broadcasted_iota(jnp.int32, (BLK, BLK), 0)
    col = lax.broadcasted_iota(jnp.int32, (BLK, BLK), 1)
    swapped = TOK * s_ref[0]
    place = lax.rem(row + swapped, BLK) <= lax.rem(col + swapped, BLK)
    tri = jnp.where(place, 0.0, -jnp.inf)
    scores[:BLK] += jnp.concatenate([tri] * GROUP, 1)


def probs_kernel(
    s_ref, qo, qr, go, gr, k0, k1, k2, k3, k4, key_seg, query_seg,
    shift, d0, d1, d2, d3, d4, keys, queries, scores, weights,
):
    score_all(s_ref, qo, qr, (k0, k1, k2, k3, k4), key_seg, query_seg, keys, queries, scores)
    largest = jnp.full((8, ROWS), -jnp.inf, F32)
    for rows in chunks():
        largest = jnp.maximum(largest, fold(scores[rows], jnp.max))
    largest = jnp.max(largest, axis=0, keepdims=True)
    total = jnp.zeros((8, ROWS), F32)
    for rows in chunks():
        e = jnp.exp((scores[rows] - largest) * SCALE)
        total += fold(e, jnp.sum)
        weights[rows] = e.astype(BF)
    total = jnp.sum(total, axis=0, keepdims=True)
    shift[0] = jnp.broadcast_to(largest * SCALE + jnp.log(total), (8, ROWS))
    inverse = jnp.broadcast_to(1.0 / total, (8, ROWS)).T[:, :1]
    g = (heads_of(go, gr).astype(F32) * inverse).astype(BF)
    part = jnp.dot(weights[...], g, preferred_element_type=F32)
    for i, out in enumerate((d0, d1, d2, d3, d4)):
        out[...] = part[i * BLK : (i + 1) * BLK].astype(out.dtype)


def grads_kernel(
    s_ref, qo, qr, go, gr, k0, k1, k2, k3, k4, v0, v1, v2, v3, v4, key_seg, query_seg, shift,
    dqo, dqr, d0, d1, d2, d3, d4, keys, queries, scores, key_t, values, grad_probs, grad_scores,
):
    score_all(s_ref, qo, qr, (k0, k1, k2, k3, k4), key_seg, query_seg, keys, queries, scores)
    for i, (k, v) in enumerate(zip((k0, k1, k2, k3, k4), (v0, v1, v2, v3, v4))):
        key_t[:, i * BLK : (i + 1) * BLK] = k[...].T
        values[i * BLK : (i + 1) * BLK] = v[...]
    grad_probs[...] = lax.dot_general(
        values[...], heads_of(go, gr), NT, preferred_element_type=F32
    )
    row_terms = jnp.zeros((8, ROWS), F32)
    for rows in chunks():
        p = jnp.exp(scores[rows] * SCALE - shift[0, :1])
        scores[rows] = p
        row_terms += fold(p * grad_probs[rows], jnp.sum)
    row_terms = jnp.sum(row_terms, axis=0, keepdims=True)
    for rows in chunks():
        grad_scores[rows] = (scores[rows] * (grad_probs[rows] - row_terms)).astype(BF)
    part = jnp.dot(grad_scores[...], heads_of(qo, qr), preferred_element_type=F32)
    dq = jnp.dot(key_t[...], grad_scores[...], preferred_element_type=F32)
    dq = (dq * SCALE).T.astype(BF)
    for h in range(GROUP):
        cols = slice(h * HEAD, (h + 1) * HEAD)
        dqo[:, cols] = dq[h * BLK : h * BLK + TOK]
        dqr[:, cols] = dq[h * BLK + TOK : (h + 1) * BLK]
    for i, out in enumerate((d0, d1, d2, d3, d4)):
        out[...] = (part[i * BLK : (i + 1) * BLK] * SCALE).astype(out.dtype)


def own_spec():
    return pl.BlockSpec((TOK, GROUP * HEAD), lambda j, s: (0, s[0] * 2 + j))


def recv_spec():
    return pl.BlockSpec((TOK, GROUP * HEAD), lambda j, s: (0, j))


def window_specs():
    second = pl.BlockSpec((BLK, HEAD), lambda j, s: (1, j))
    return [block_spec(), block_spec(), block_spec(), second, block_spec()]


def block_spec():
    return pl.BlockSpec((BLK, HEAD), lambda j, s: (0, j))


def same_spec(*shape):
    return pl.BlockSpec(shape, lambda j, s: (0, 0))


def shift_spec():
    return pl.BlockSpec((1, 8, ROWS), lambda j, s: (j, 0, 0))


def code_specs():
    return [same_spec(1, WIN), same_spec(1, BLK)]


def score_scratch():
    return [
        pltpu.VMEM((WIN, 2 * HEAD), BF),
        pltpu.VMEM((ROWS, 2 * HEAD), BF),
        pltpu.VMEM((WIN, ROWS), F32),
    ]


def vmem_spec():
    return pl.BlockSpec(memory_space=pltpu.VMEM)


def window_outs():
    first = jax.ShapeDtypeStruct((BLK, 2 * HEAD), F32)
    return [first] + [jax.ShapeDtypeStruct((BLK, 2 * HEAD), BF)] * BACK


def run_probs(place, qo, qr, go, gr, keys, codes):
    outs = pl.pallas_call(
        probs_kernel,
        grid_spec=pltpu.PrefetchScalarGridSpec(
            num_scalar_prefetch=1,
            grid=(2,),
            in_specs=[own_spec(), recv_spec(), own_spec(), recv_spec()]
            + window_specs()
            + code_specs(),
            out_specs=[shift_spec()] + [block_spec()] * (BACK + 1),
            scratch_shapes=score_scratch() + [pltpu.VMEM((WIN, ROWS), BF)],
        ),
        out_shape=[jax.ShapeDtypeStruct((2, 8, ROWS), F32)] + window_outs(),
        compiler_params=pltpu.CompilerParams(vmem_limit_bytes=VMEM),
        cost_estimate=pl.CostEstimate(
            flops=2 * 3 * 16 * WIN * BLK * HEAD,
            bytes_accessed=16 << 20,
            transcendentals=16 * WIN * BLK,
        ),
        name="probs",
    )(place, qo, qr, go, gr, *keys, *codes)
    return outs[0], outs[1:]


def run_grads(place, qo, qr, go, gr, keys, values, codes, shift):
    outs = pl.pallas_call(
        grads_kernel,
        grid_spec=pltpu.PrefetchScalarGridSpec(
            num_scalar_prefetch=1,
            grid=(2,),
            in_specs=[own_spec(), recv_spec(), own_spec(), recv_spec()]
            + window_specs()
            + window_specs()
            + code_specs()
            + [shift_spec()],
            out_specs=[recv_spec(), recv_spec()] + [block_spec()] * (BACK + 1),
            scratch_shapes=score_scratch()
            + [
                pltpu.VMEM((HEAD, WIN), BF),
                pltpu.VMEM((WIN, HEAD), BF),
                pltpu.VMEM((WIN, ROWS), F32),
                pltpu.VMEM((WIN, ROWS), BF),
            ],
        ),
        out_shape=[jax.ShapeDtypeStruct((TOK, 16 * HEAD), BF)] * 2 + window_outs(),
        compiler_params=pltpu.CompilerParams(vmem_limit_bytes=VMEM),
        cost_estimate=pl.CostEstimate(
            flops=2 * 5 * 16 * WIN * BLK * HEAD,
            bytes_accessed=16 << 20,
            transcendentals=16 * WIN * BLK,
        ),
        name="grads",
    )(place, qo, qr, go, gr, *keys, *values, *codes, shift)
    return outs[0], outs[1], outs[2:]


def weight_kernel(s_ref, xo, xr, mine, theirs, out):
    x, c = s_ref[1], s_ref[2]
    total = jnp.zeros((xo.shape[1], 2 * HEAD), F32)
    for other, ref in ((0, mine), (1, theirs)):
        core = c if other == 0 else 1 - c
        for d in range(4):
            seq = lax.rem(x - d + 4, 4) * 2 + core
            total += jnp.dot(xo[seq], ref[d, :TOK], preferred_element_type=F32)
            total += jnp.dot(xr[seq], ref[d, TOK:], preferred_element_type=F32)
    out[...] = total.astype(out.dtype)


def run_weight(place, xo, xr, mine, theirs):
    return pl.pallas_call(
        weight_kernel,
        in_specs=[pl.BlockSpec(memory_space=pltpu.SMEM)] + [vmem_spec()] * 4,
        out_specs=vmem_spec(),
        out_shape=jax.ShapeDtypeStruct((xo.shape[1], 2 * HEAD), BF),
        compiler_params=pltpu.CompilerParams(vmem_limit_bytes=16 << 20),
        cost_estimate=pl.CostEstimate(
            flops=2 * 2048 * 640 * 256, bytes_accessed=4 << 20, transcendentals=0
        ),
        name="weight",
    )(place, xo, xr, mine, theirs)


def after(value, *others):
    return lax.optimization_barrier((value, *others))


def small_call(kernel, out_shape, name, args, tokens=()):
    def run(*refs):
        kernel(*refs[: len(args)], *refs[len(args) + len(tokens) :])

    return pl.pallas_call(
        run,
        in_specs=[vmem_spec()] * len(args) + [pl.BlockSpec(memory_space=pl.ANY)] * len(tokens),
        out_specs=vmem_spec(),
        out_shape=out_shape,
        compiler_params=pltpu.CompilerParams(vmem_limit_bytes=16 << 20),
        cost_estimate=pl.CostEstimate(flops=0, bytes_accessed=2 << 20, transcendentals=0),
        name=name,
    )(*args, *tokens)


def sum_kernel(first, a, b, c, d, out):
    total = first[...] + a[...].astype(F32) + b[...].astype(F32)
    out[...] = (total + c[...].astype(F32) + d[...].astype(F32)).astype(BF)


def body(sizes, query, key, value, grad, layer_input, segment_ids):
    nz = sizes["z"]
    z, yl, x, c = (lax.axis_index(a) for a in ("z", "yl", "x", "c"))
    place = jnp.stack([yl, x, c, z]).astype(jnp.int32)
    q, k, v, g, xin, seg = (a[0] for a in (query, key, value, grad, layer_input, segment_ids))
    swap = [(0, 1), (1, 0)]

    def half(a, which, width):
        return lax.dynamic_slice_in_dim(a, which * width, width, 1)

    def to_pair(a):
        return lax.ppermute(a, "yl", swap)

    kv_send = jnp.concatenate([half(k, 1 - yl, 256), half(v, 1 - yl, 256)], 1)
    kv_send, q, g, xin = after(kv_send, q, g, xin)
    kv_recv = to_pair(kv_send)
    q_recv = to_pair(half(q, 1 - yl, 2048))
    g_recv = to_pair(half(g, 1 - yl, 2048))

    def fetch_first(own):
        one = lax.ppermute(own, "z", [(i, i + 1) for i in range(nz - 1)])
        round_first = [(i, (i - 2) % nz) for i in range(nz - BACK)]
        return one, lax.ppermute(own, "z", round_first)

    def fetch_rest(own, one, half_way):
        both = jnp.concatenate([own, one], 0)
        both = lax.ppermute(both, "z", [(i, i + 2) for i in range(nz - 2)])
        round_rest = [((i - 2) % nz, (i - 4) % nz) for i in range(nz - BACK)]
        return [own, one, both, both, lax.ppermute(half_way, "z", round_rest)]

    own_keys = jnp.concatenate([half(k, yl, 256), kv_recv[:, :256]], 0)
    own_values = jnp.concatenate([half(v, yl, 256), kv_recv[:, 256:]], 0)
    first_keys = fetch_first(own_keys)
    keys = fetch_rest(own_keys, *first_keys)
    next_value = lax.ppermute(own_values, "z", [(i, i + 1) for i in range(nz - 1)])
    far_value = lax.ppermute(own_values, "z", [(i, i + BACK) for i in range(nz - BACK)])
    both = jnp.concatenate([own_values, next_value], 0)
    both = lax.ppermute(both, "z", [(i, i + 2) for i in range(nz - 2)])
    values = [own_values, next_value, both, both, far_value]

    groups = 8
    x_t = xin.T
    width = x_t.shape[0] // groups
    rows = width // 32
    x_t = x_t.reshape(32, groups, rows, TOK).transpose(1, 0, 2, 3).reshape(groups * width, TOK)
    x_own = lax.all_to_all(x_t, ("x", "c"), split_axis=0, concat_axis=0, tiled=True)
    x_own, q_recv, g_recv = after(x_own, q_recv, g_recv)
    x_own = x_own.reshape(groups, width, TOK)
    x_recv = to_pair(x_own)

    padded = jnp.concatenate([jnp.full((BACK * BLK,), -1, jnp.int32), seg])
    window = lax.dynamic_slice_in_dim(padded, z * BLK, WIN).reshape(BACK + 1, 2, TOK)[::-1]
    window = jnp.where(yl == 0, window, window[:, ::-1])
    key_seg = window.reshape(1, WIN)
    query_seg = window[0].reshape(1, BLK)

    def travel(parts):
        sent = []
        for d in range(1, BACK + 1):
            sent.append(lax.ppermute(parts[d], "z", [(i, i - d) for i in range(d, nz)]))
        return sent

    def add_up(first, rest):
        for a in rest:
            first = first + a.astype(F32)
        return first.astype(BF)

    codes = (key_seg, query_seg)
    shift, value_parts = run_probs(place, q, q_recv, g, g_recv, keys, codes)
    value_sent = travel(value_parts)
    dq_own, dq_far, key_parts = run_grads(
        place, q, q_recv, g, g_recv, keys, values, codes, shift
    )
    value_first, dq_far, key_parts, *value_sent = after(
        value_parts[0], dq_far, key_parts, *value_sent
    )
    value_low = add_up(value_first, value_sent)

    near = [value_low]
    for d in range(1, 4):
        near.append(lax.ppermute(value_low, "x", [(i, (i + d) % 4) for i in range(4)]))
    near = jnp.stack(near)
    far = lax.ppermute(near, "c", swap)
    part = run_weight(place, x_own, x_recv, near, far)
    dq_recv = to_pair(dq_far)
    key_sent = travel(key_parts)
    key_block = jax.ShapeDtypeStruct((BLK, 2 * HEAD), BF)
    key_low = small_call(sum_kernel, key_block, "key_sum", (key_parts[0], *key_sent), (part,))
    part = lax.all_to_all(
        part.reshape(32, rows, 256), ("z", "yl", "yh"), split_axis=0, concat_axis=0, tiled=True
    )
    total = part.reshape(nz, 2, 2, rows, 256).astype(F32).sum(axis=(0, 2))
    total = jnp.concatenate([total[0], total[1]], axis=1)
    weight = total * (1.0 / math.sqrt(16 * 2048))

    def join(mine, theirs):
        return jnp.where(
            yl == 0,
            jnp.concatenate([mine, theirs], 1),
            jnp.concatenate([theirs, mine], 1),
        )

    dq = join(dq_own, dq_recv)
    dk = join(key_low[:TOK], to_pair(key_low[TOK:]))
    return dq[None], dk[None], weight


def solution(mesh):
    fine = Mesh(mesh.devices.reshape(8, 2, 2, 4, 2), ("z", "yl", "yh", "x", "c"))
    sizes = dict(fine.shape)
    tokens = P(("yh", "x", "c"), ("z", "yl"), None)
    return jax.shard_map(
        functools.partial(body, sizes),
        mesh=fine,
        in_specs=(tokens,) * 5 + (P(("yh", "x", "c"), None),),
        out_specs=(tokens, tokens, P(("z", "yl", "yh", "x", "c"), None)),
        check_vma=False,
    )
```

```python
import functools
import math

import jax
import jax.numpy as jnp
from jax import lax
from jax.experimental import pallas as pl
from jax.experimental.pallas import tpu as pltpu
from jax.sharding import Mesh
from jax.sharding import PartitionSpec as P

HEAD = 128
SCALE = 1.0 / math.sqrt(HEAD)
BF = jnp.bfloat16
F32 = jnp.float32
BACK = 4
TOK = 128
BLK = 256
WIN = (BACK + 1) * BLK
GROUP = 8
ROWS = GROUP * BLK
CHUNK = 64
VMEM = 56 * 1024 * 1024
FAR = -(2.0**100)
NT = (((1,), (1,)), ((), ()))


def heads_of(own_ref, recv_ref):
    rows = []
    for h in range(GROUP):
        cols = slice(h * HEAD, (h + 1) * HEAD)
        rows += [own_ref[:, cols], recv_ref[:, cols]]
    return jnp.concatenate(rows, axis=0)


def fold(a, op):
    return op(a.reshape(a.shape[0] // 8, 8, a.shape[1]), axis=0)


def chunks():
    return [slice(c, c + CHUNK) for c in range(0, WIN, CHUNK)]


def score_all(s_ref, qo, qr, blocks, key_seg, query_seg, keys, queries, scores):
    lanes = lax.broadcasted_iota(jnp.int32, (1, HEAD), 1)
    for i, k in enumerate(blocks):
        rows = slice(i * BLK, (i + 1) * BLK)
        keys[rows, :HEAD] = k[...]
        seg = jnp.broadcast_to(key_seg[:, rows], (8, BLK)).T[:, :1]
        keys[rows, HEAD:] = jnp.where((lanes < 4) & (seg != lanes), FAR, 0.0).astype(BF)
    queries[:, :HEAD] = heads_of(qo, qr)
    query_code = jnp.broadcast_to(query_seg[...], (8, BLK)).T[:, :1] == lanes
    query_code = query_code.astype(BF)
    for h in range(GROUP):
        queries[h * BLK : (h + 1) * BLK, HEAD:] = query_code
    scores[...] = lax.dot_general(keys[...], queries[...], NT, preferred_element_type=F32)
    row = lax.broadcasted_iota(jnp.int32, (BLK, BLK), 0)
    col = lax.broadcasted_iota(jnp.int32, (BLK, BLK), 1)
    swapped = TOK * s_ref[0]
    place = lax.rem(row + swapped, BLK) <= lax.rem(col + swapped, BLK)
    tri = jnp.where(place, 0.0, -jnp.inf)
    scores[:BLK] += jnp.concatenate([tri] * GROUP, 1)


def probs_kernel(
    s_ref, qo, qr, go, gr, k0, k1, k2, k3, k4, key_seg, query_seg,
    shift, d0, d1, d2, d3, d4, keys, queries, scores, weights,
):
    score_all(s_ref, qo, qr, (k0, k1, k2, k3, k4), key_seg, query_seg, keys, queries, scores)
    largest = jnp.full((8, ROWS), -jnp.inf, F32)
    for rows in chunks():
        largest = jnp.maximum(largest, fold(scores[rows], jnp.max))
    largest = jnp.max(largest, axis=0, keepdims=True)
    total = jnp.zeros((8, ROWS), F32)
    for rows in chunks():
        e = jnp.exp((scores[rows] - largest) * SCALE)
        total += fold(e, jnp.sum)
        weights[rows] = e.astype(BF)
    total = jnp.sum(total, axis=0, keepdims=True)
    shift[0] = jnp.broadcast_to(largest * SCALE + jnp.log(total), (8, ROWS))
    inverse = jnp.broadcast_to(1.0 / total, (8, ROWS)).T[:, :1]
    g = (heads_of(go, gr).astype(F32) * inverse).astype(BF)
    part = jnp.dot(weights[...], g, preferred_element_type=F32)
    for i, out in enumerate((d0, d1, d2, d3, d4)):
        out[...] = part[i * BLK : (i + 1) * BLK].astype(out.dtype)


def grads_kernel(
    s_ref, qo, qr, go, gr, k0, k1, k2, k3, k4, v0, v1, v2, v3, v4, key_seg, query_seg, shift,
    dqo, dqr, d0, d1, d2, d3, d4, keys, queries, scores, key_t, values, grad_probs, grad_scores,
):
    score_all(s_ref, qo, qr, (k0, k1, k2, k3, k4), key_seg, query_seg, keys, queries, scores)
    for i, (k, v) in enumerate(zip((k0, k1, k2, k3, k4), (v0, v1, v2, v3, v4))):
        key_t[:, i * BLK : (i + 1) * BLK] = k[...].T
        values[i * BLK : (i + 1) * BLK] = v[...]
    grad_probs[...] = lax.dot_general(
        values[...], heads_of(go, gr), NT, preferred_element_type=F32
    )
    row_terms = jnp.zeros((8, ROWS), F32)
    for rows in chunks():
        p = jnp.exp(scores[rows] * SCALE - shift[0, :1])
        scores[rows] = p
        row_terms += fold(p * grad_probs[rows], jnp.sum)
    row_terms = jnp.sum(row_terms, axis=0, keepdims=True)
    for rows in chunks():
        grad_scores[rows] = (scores[rows] * (grad_probs[rows] - row_terms)).astype(BF)
    part = jnp.dot(grad_scores[...], heads_of(qo, qr), preferred_element_type=F32)
    dq = jnp.dot(key_t[...], grad_scores[...], preferred_element_type=F32)
    dq = (dq * SCALE).T.astype(BF)
    for h in range(GROUP):
        cols = slice(h * HEAD, (h + 1) * HEAD)
        dqo[:, cols] = dq[h * BLK : h * BLK + TOK]
        dqr[:, cols] = dq[h * BLK + TOK : (h + 1) * BLK]
    for i, out in enumerate((d0, d1, d2, d3, d4)):
        out[...] = (part[i * BLK : (i + 1) * BLK] * SCALE).astype(out.dtype)


def own_spec():
    return pl.BlockSpec((TOK, GROUP * HEAD), lambda j, s: (0, s[0] * 2 + j))


def recv_spec():
    return pl.BlockSpec((TOK, GROUP * HEAD), lambda j, s: (0, j))


def window_specs():
    second = pl.BlockSpec((BLK, HEAD), lambda j, s: (1, j))
    return [block_spec(), block_spec(), block_spec(), second, block_spec()]


def block_spec():
    return pl.BlockSpec((BLK, HEAD), lambda j, s: (0, j))


def same_spec(*shape):
    return pl.BlockSpec(shape, lambda j, s: (0, 0))


def shift_spec():
    return pl.BlockSpec((1, 8, ROWS), lambda j, s: (j, 0, 0))


def code_specs():
    return [same_spec(1, WIN), same_spec(1, BLK)]


def score_scratch():
    return [
        pltpu.VMEM((WIN, 2 * HEAD), BF),
        pltpu.VMEM((ROWS, 2 * HEAD), BF),
        pltpu.VMEM((WIN, ROWS), F32),
    ]


def vmem_spec():
    return pl.BlockSpec(memory_space=pltpu.VMEM)


def window_outs():
    first = jax.ShapeDtypeStruct((BLK, 2 * HEAD), F32)
    return [first] + [jax.ShapeDtypeStruct((BLK, 2 * HEAD), BF)] * BACK


def run_probs(place, qo, qr, go, gr, keys, codes):
    outs = pl.pallas_call(
        probs_kernel,
        grid_spec=pltpu.PrefetchScalarGridSpec(
            num_scalar_prefetch=1,
            grid=(2,),
            in_specs=[own_spec(), recv_spec(), own_spec(), recv_spec()]
            + window_specs()
            + code_specs(),
            out_specs=[shift_spec()] + [block_spec()] * (BACK + 1),
            scratch_shapes=score_scratch() + [pltpu.VMEM((WIN, ROWS), BF)],
        ),
        out_shape=[jax.ShapeDtypeStruct((2, 8, ROWS), F32)] + window_outs(),
        compiler_params=pltpu.CompilerParams(vmem_limit_bytes=VMEM),
        cost_estimate=pl.CostEstimate(
            flops=2 * 3 * 16 * WIN * BLK * HEAD,
            bytes_accessed=16 << 20,
            transcendentals=16 * WIN * BLK,
        ),
        name="probs",
    )(place, qo, qr, go, gr, *keys, *codes)
    return outs[0], outs[1:]


def run_grads(place, qo, qr, go, gr, keys, values, codes, shift):
    outs = pl.pallas_call(
        grads_kernel,
        grid_spec=pltpu.PrefetchScalarGridSpec(
            num_scalar_prefetch=1,
            grid=(2,),
            in_specs=[own_spec(), recv_spec(), own_spec(), recv_spec()]
            + window_specs()
            + window_specs()
            + code_specs()
            + [shift_spec()],
            out_specs=[recv_spec(), recv_spec()] + [block_spec()] * (BACK + 1),
            scratch_shapes=score_scratch()
            + [
                pltpu.VMEM((HEAD, WIN), BF),
                pltpu.VMEM((WIN, HEAD), BF),
                pltpu.VMEM((WIN, ROWS), F32),
                pltpu.VMEM((WIN, ROWS), BF),
            ],
        ),
        out_shape=[jax.ShapeDtypeStruct((TOK, 16 * HEAD), BF)] * 2 + window_outs(),
        compiler_params=pltpu.CompilerParams(vmem_limit_bytes=VMEM),
        cost_estimate=pl.CostEstimate(
            flops=2 * 5 * 16 * WIN * BLK * HEAD,
            bytes_accessed=16 << 20,
            transcendentals=16 * WIN * BLK,
        ),
        name="grads",
    )(place, qo, qr, go, gr, *keys, *values, *codes, shift)
    return outs[0], outs[1], outs[2:]


def weight_kernel(s_ref, xo, xr, mine, theirs, out):
    x, c = s_ref[1], s_ref[2]
    total = jnp.zeros((xo.shape[1], 2 * HEAD), F32)
    for other, ref in ((0, mine), (1, theirs)):
        core = c if other == 0 else 1 - c
        for d in range(4):
            seq = lax.rem(x - d + 4, 4) * 2 + core
            total += jnp.dot(xo[seq], ref[d, :TOK], preferred_element_type=F32)
            total += jnp.dot(xr[seq], ref[d, TOK:], preferred_element_type=F32)
    out[...] = total.astype(out.dtype)


def run_weight(place, xo, xr, mine, theirs):
    return pl.pallas_call(
        weight_kernel,
        in_specs=[pl.BlockSpec(memory_space=pltpu.SMEM)] + [vmem_spec()] * 4,
        out_specs=vmem_spec(),
        out_shape=jax.ShapeDtypeStruct((xo.shape[1], 2 * HEAD), BF),
        compiler_params=pltpu.CompilerParams(vmem_limit_bytes=16 << 20),
        cost_estimate=pl.CostEstimate(
            flops=2 * 2048 * 640 * 256, bytes_accessed=4 << 20, transcendentals=0
        ),
        name="weight",
    )(place, xo, xr, mine, theirs)


def after(value, *others):
    return lax.optimization_barrier((value, *others))


def small_call(kernel, out_shape, name, args, tokens=()):
    def run(*refs):
        kernel(*refs[: len(args)], *refs[len(args) + len(tokens) :])

    return pl.pallas_call(
        run,
        in_specs=[vmem_spec()] * len(args) + [pl.BlockSpec(memory_space=pl.ANY)] * len(tokens),
        out_specs=vmem_spec(),
        out_shape=out_shape,
        compiler_params=pltpu.CompilerParams(vmem_limit_bytes=16 << 20),
        cost_estimate=pl.CostEstimate(flops=0, bytes_accessed=2 << 20, transcendentals=0),
        name=name,
    )(*args, *tokens)


def sum_kernel(first, a, b, c, d, out):
    total = first[...] + a[...].astype(F32) + b[...].astype(F32)
    out[...] = (total + c[...].astype(F32) + d[...].astype(F32)).astype(BF)


def body(sizes, query, key, value, grad, layer_input, segment_ids):
    nz = sizes["z"]
    z, yl, x, c = (lax.axis_index(a) for a in ("z", "yl", "x", "c"))
    place = jnp.stack([yl, x, c, z]).astype(jnp.int32)
    q, k, v, g, xin, seg = (a[0] for a in (query, key, value, grad, layer_input, segment_ids))
    swap = [(0, 1), (1, 0)]

    def half(a, which, width):
        return lax.dynamic_slice_in_dim(a, which * width, width, 1)

    def to_pair(a):
        return lax.ppermute(a, "yl", swap)

    kv_send = jnp.concatenate([half(k, 1 - yl, 256), half(v, 1 - yl, 256)], 1)
    kv_send, q, g, xin = after(kv_send, q, g, xin)
    kv_recv = to_pair(kv_send)
    q_recv = to_pair(half(q, 1 - yl, 2048))
    g_recv = to_pair(half(g, 1 - yl, 2048))

    def fetch_first(own):
        one = lax.ppermute(own, "z", [(i, i + 1) for i in range(nz - 1)])
        round_first = [(i, (i - 2) % nz) for i in range(nz - BACK)]
        return one, lax.ppermute(own, "z", round_first)

    def fetch_rest(own, one, half_way):
        both = jnp.concatenate([own, one], 0)
        both = lax.ppermute(both, "z", [(i, i + 2) for i in range(nz - 2)])
        round_rest = [((i - 2) % nz, (i - 4) % nz) for i in range(nz - BACK)]
        return [own, one, both, both, lax.ppermute(half_way, "z", round_rest)]

    own_keys = jnp.concatenate([half(k, yl, 256), kv_recv[:, :256]], 0)
    own_values = jnp.concatenate([half(v, yl, 256), kv_recv[:, 256:]], 0)
    first_keys = fetch_first(own_keys)
    keys = fetch_rest(own_keys, *first_keys)
    next_value = lax.ppermute(own_values, "z", [(i, i + 1) for i in range(nz - 1)])
    far_value = lax.ppermute(own_values, "z", [(i, i + BACK) for i in range(nz - BACK)])
    both = jnp.concatenate([own_values, next_value], 0)
    both = lax.ppermute(both, "z", [(i, i + 2) for i in range(nz - 2)])
    values = [own_values, next_value, both, both, far_value]

    groups = 8
    x_t = xin.T
    width = x_t.shape[0] // groups
    rows = width // 32
    x_t = x_t.reshape(32, groups, rows, TOK).transpose(1, 0, 2, 3).reshape(groups * width, TOK)
    x_own = lax.all_to_all(x_t, ("x", "c"), split_axis=0, concat_axis=0, tiled=True)
    x_own, q_recv, g_recv = after(x_own, q_recv, g_recv)
    x_own = x_own.reshape(groups, width, TOK)
    x_recv = to_pair(x_own)

    padded = jnp.concatenate([jnp.full((BACK * BLK,), -1, jnp.int32), seg])
    window = lax.dynamic_slice_in_dim(padded, z * BLK, WIN).reshape(BACK + 1, 2, TOK)[::-1]
    window = jnp.where(yl == 0, window, window[:, ::-1])
    key_seg = window.reshape(1, WIN)
    query_seg = window[0].reshape(1, BLK)

    def travel(parts):
        sent = []
        for d in range(BACK, 0, -1):
            sent.append(lax.ppermute(parts[d], "z", [(i, i - d) for i in range(d, nz)]))
        return sent

    def add_up(first, rest):
        for a in rest:
            first = first + a.astype(F32)
        return first.astype(BF)

    codes = (key_seg, query_seg)
    shift, value_parts = run_probs(place, q, q_recv, g, g_recv, keys, codes)
    value_sent = travel(value_parts)
    dq_own, dq_far, key_parts = run_grads(
        place, q, q_recv, g, g_recv, keys, values, codes, shift
    )
    value_first, dq_far, *value_sent = after(value_parts[0], dq_far, *value_sent)
    value_low = add_up(value_first, value_sent)

    near = [value_low]
    for d in range(1, 4):
        near.append(lax.ppermute(value_low, "x", [(i, (i + d) % 4) for i in range(4)]))
    near = jnp.stack(near)
    far = lax.ppermute(near, "c", swap)
    part = run_weight(place, x_own, x_recv, near, far)
    dq_recv = to_pair(dq_far)
    key_sent = travel(key_parts)
    key_block = jax.ShapeDtypeStruct((BLK, 2 * HEAD), BF)
    key_low = small_call(sum_kernel, key_block, "key_sum", (key_parts[0], *key_sent), (part,))
    part = lax.all_to_all(
        part.reshape(32, rows, 256), ("z", "yl", "yh"), split_axis=0, concat_axis=0, tiled=True
    )
    total = part.reshape(nz, 2, 2, rows, 256).astype(F32).sum(axis=(0, 2))
    total = jnp.concatenate([total[0], total[1]], axis=1)
    weight = total * (1.0 / math.sqrt(16 * 2048))

    def join(mine, theirs):
        return jnp.where(
            yl == 0,
            jnp.concatenate([mine, theirs], 1),
            jnp.concatenate([theirs, mine], 1),
        )

    dq = join(dq_own, dq_recv)
    dk = join(key_low[:TOK], to_pair(key_low[TOK:]))
    return dq[None], dk[None], weight


def solution(mesh):
    fine = Mesh(mesh.devices.reshape(8, 2, 2, 4, 2), ("z", "yl", "yh", "x", "c"))
    sizes = dict(fine.shape)
    tokens = P(("yh", "x", "c"), ("z", "yl"), None)
    return jax.shard_map(
        functools.partial(body, sizes),
        mesh=fine,
        in_specs=(tokens,) * 5 + (P(("yh", "x", "c"), None),),
        out_specs=(tokens, tokens, P(("z", "yl", "yh", "x", "c"), None)),
        check_vma=False,
    )
```
